1024 devices in a mesh: vp: 128 (over z, y), op: 8 (over x, core).
Axes of the slice: x: 4, y: 4, z: 32, core: 2. Of those that a mesh axis runs over, the one named last changes fastest.
Arguments:
- amplitudes: float32 [512, 16384], P('op', 'vp'), may hold values from -6 to 6
- integrals: float32 [128, 32, 128, 128], P('vp', None, 'op'), may hold values from -0.09375 to 0.09375
- rest: float32 [512, 16384], P('op', 'vp'), may hold values from -6 to 6
- occ_energy: float32 [512], P('op'), may hold values from -3 to -0.5
- vir_energy: float32 [16384], P('vp'), may hold values from 0.5 to 6
- block_irrep: int32 [128], replicated, may hold values from 0 to 7, as said below
Outputs:
- new_amplitudes: float32 [512, 16384], P('op', 'vp')
The draws below stay inside these ranges and needn't reach their ends.
Inputs may be any that keep to these rules, and one draw needn't show every extreme that they name: `block_irrep`: no irrep labels more than 32 blocks, and one labels exactly 32; slots k of integrals[position[b]] at or past count[b] are not used.
All inputs are finite; a program needn't handle non-finite values.
Results may differ from the reference program's by a relative error of at most 0.0003.
Values sent between devices are 32-bit elements; how exact they have to be, the bound alone decides.
No kernel may reach another device: no remote copies, remote signals or barrier semaphores. Data moves between devices by JAX's collectives and lax.ppermute only.
A program may use at most 32 MiB of HBM per device.

```python
import jax
import jax.numpy as jnp
from jax import lax

BS = 128
IRREPS = 8
NBLK = 128
PAIRS = 16384
KMAX = 32
IJ = 512


def draw_block_irrep(key, part):
    key = jax.random.fold_in(key, 11)
    order_key, name_key = jax.random.split(key)
    order = jax.random.permutation(order_key, NBLK)
    others = 1 + (order - KMAX) * (IRREPS - 1) // (NBLK - KMAX)
    base = jnp.where(order < KMAX, 0, others).astype(jnp.int32)
    names = jax.random.permutation(name_key, IRREPS).astype(jnp.int32)
    return jnp.take(names, base).astype(jnp.int32)


def shard_levels(own_key, shape, cuts, smallest, top_value):
    factor_of, own = 1.0, jax.random.fold_in(own_key, 6)
    for axis_at, parts in cuts:
        draws = jnp.exp(jax.random.uniform(jax.random.fold_in(own, axis_at), (parts,), jnp.float32, smallest / len(cuts), top_value / len(cuts)))
        factor_of = factor_of * jnp.repeat(draws, shape[axis_at] // parts).reshape([-1 if axis == axis_at else 1 for axis in range(len(shape))])
    return factor_of


def normal_values(key, shape, width, bound, cuts=(), kind=jnp.bfloat16):
    array = width * jax.random.normal(key, shape, jnp.float32)
    if cuts:
        array = array * shard_levels(key, shape, cuts, -0.22, 0.18)
    return jnp.clip(array, -bound, bound).astype(kind)


def setup_inputs(seed: int = 0) -> dict:
    arg_keys = jax.random.split(jax.random.key(seed), 7)
    amplitudes = normal_values(arg_keys[0], (IJ, PAIRS), 1.0, 6.0, ((0, 8), (1, 128)), jnp.float32)
    integrals = normal_values(arg_keys[1], (NBLK, KMAX, BS, BS), (KMAX * BS) ** -0.5, 0.09375, ((0, 128), (2, 8)), jnp.float32)
    rest = normal_values(arg_keys[2], (IJ, PAIRS), 1.0, 6.0, ((0, 8), (1, 128)), jnp.float32)
    occ_energy = jnp.clip(-3.0 + 2.5 * jax.random.uniform(arg_keys[3], (IJ,), jnp.float32) ** shard_levels(arg_keys[3], (IJ,), ((0, 8),), -0.2, 0.2), -3.0, -0.5)
    vir_energy = jnp.clip(0.5 + 5.5 * jax.random.uniform(arg_keys[4], (PAIRS,), jnp.float32) ** shard_levels(arg_keys[4], (PAIRS,), ((0, 128),), -0.2, 0.2), 0.5, 6.0)
    block_irrep = draw_block_irrep(jax.random.fold_in(arg_keys[6], 71), 0)
    return {"amplitudes": amplitudes, "integrals": integrals, "rest": rest, "occ_energy": occ_energy, "vir_energy": vir_energy, "block_irrep": block_irrep}


def coupling_tables(block_irrep):
    count_blocks = block_irrep.shape[0]
    positions = jnp.arange(count_blocks, dtype=jnp.int32)
    same = (block_irrep[:, None] == block_irrep[None, :]).astype(jnp.int32)
    earlier = (positions[None, :] < positions[:, None]).astype(jnp.int32)
    rank = jnp.sum(same * earlier, axis=1).astype(jnp.int32)
    counts = jnp.sum(same, axis=1).astype(jnp.int32)
    lower = jnp.sum((block_irrep[None, :] < block_irrep[:, None]).astype(jnp.int32), axis=1).astype(jnp.int32)
    place = (lower + rank).astype(jnp.int32)
    slots = jnp.arange(KMAX, dtype=jnp.int32)
    chosen = same[:, None, :] * (rank[None, None, :] == slots[None, :, None]).astype(jnp.int32)
    partner = jnp.sum(chosen * positions[None, None, :], axis=2).astype(jnp.int32)
    valid = (slots[None, :] < counts[:, None]).astype(jnp.float32)
    return partner, valid, place


def reference(amplitudes, integrals, rest, occ_energy, vir_energy, block_irrep):
    partner, valid, place = coupling_tables(block_irrep)
    blocks = amplitudes.reshape(IJ, NBLK, BS)

    def one_block(args):
        slot_ids, slot_mask, where = args
        weights = lax.dynamic_index_in_dim(integrals, where.astype(jnp.int32), 0, False)
        picked = jnp.take(blocks, slot_ids, axis=1) * slot_mask[None, :, None]
        return jnp.einsum("qkc,kac->qa", picked, weights, precision=lax.Precision.HIGHEST)

    ladder = lax.map(one_block, (partner, valid, place))
    ladder = jnp.transpose(ladder, (1, 0, 2)).reshape(IJ, PAIRS)
    return (ladder + rest) / (vir_energy[None, :] - occ_energy[:, None])
```

```python
import functools

import jax
import jax.numpy as jnp
from jax import lax
from jax.experimental import pallas as pl
from jax.experimental.pallas import tpu as pltpu
from jax.sharding import Mesh, PartitionSpec as P

HI, LO, Y, X, C = 8, 4, 4, 4, 2
IRREPS = 8
CLASSES = X * C
VP = ("h", "l", "y")
OP = ("x", "c")
PLANE = ("y", "x", "c")
OUT_FIRST, HOME_FIRST = 20, 16
WHOLE = pl.BlockSpec(memory_space=pltpu.VMEM)


def starts_of(irreps):
    name = lax.broadcasted_iota(jnp.int32, (IRREPS, irreps.shape[1]), 0)
    return jnp.sum((irreps < name).astype(jnp.int32), axis=1, keepdims=True)


def places_of(irreps):
    blocks = irreps.shape[1]
    own = jnp.broadcast_to(irreps.astype(jnp.float32), (blocks, blocks))
    other = own.T
    own_id = lax.broadcasted_iota(jnp.int32, (blocks, blocks), 1)
    other_id = lax.broadcasted_iota(jnp.int32, (blocks, blocks), 0)
    before = (other < own) | ((other == own) & (other_id < own_id))
    return jnp.sum(before.astype(jnp.float32), axis=0, keepdims=True).astype(jnp.int32)


def pick_rows(chosen, value):
    hot = chosen.astype(jnp.float32).astype(jnp.bfloat16)
    high, rest = split(value)
    low = (value - high.astype(jnp.float32) - rest.astype(jnp.float32)).astype(jnp.bfloat16)
    total = jnp.dot(hot, low, preferred_element_type=jnp.float32)
    total = total + jnp.dot(hot, rest, preferred_element_type=jnp.float32)
    return total + jnp.dot(hot, high, preferred_element_type=jnp.float32)


def copy_kernel(amplitudes_ref, out_ref):
    for hi in range(HI):
        out_ref[hi] = amplitudes_ref[...]


def roll_kernel(irreps_ref, integrals_ref, keep_ref, give_ref):
    starts = starts_of(irreps_ref[...])
    here = lax.axis_index(VP)
    mine = lax.axis_index(OP)
    first = jnp.max(jnp.where(starts <= here, starts, 0))
    for core, out_ref in enumerate((keep_ref, give_ref)):
        for d in range(X):
            slot = ((mine ^ (d * C + core)) - first) & (CLASSES - 1)
            for turn in range(out_ref.shape[1]):
                out_ref[d, turn] = integrals_ref[turn * CLASSES + slot]


def spread_kernel(irreps_ref, blocks_ref, _, __, out_ref, *, share):
    blocks = irreps_ref.shape[1]
    held = blocks // CLASSES
    row = lax.broadcasted_iota(jnp.int32, (blocks, blocks), 0)
    position = (row % held) * CLASSES + row // held
    sources = pltpu.roll(places_of(irreps_ref[...]), blocks - OUT_FIRST * Y, 1)
    chosen = sources == position
    for r in range(share):
        picked = pick_rows(chosen, blocks_ref[pl.ds(r, blocks, stride=share), :]).reshape(CLASSES, held, -1)
        for column in range(Y):
            out_ref[column, :, pl.ds(r * held, held), :] = picked


def split(value):
    high = value.astype(jnp.bfloat16)
    return high, (value - high.astype(jnp.float32)).astype(jnp.bfloat16)


def dot_nt(a, b):
    return lax.dot_general(a, b, (((1,), (1,)), ((), ())), preferred_element_type=jnp.float32)


def ladder_kernel(irreps_ref, blocks_ref, *refs, sources, held, share):
    weights_refs, out_ref = refs[:-1], refs[-1]
    blocks = irreps_ref.shape[1]
    turns, width = weights_refs[0].shape[1], weights_refs[0].shape[3]
    starts = starts_of(irreps_ref[...])
    mine = lax.axis_index(OP)
    for step, weights_ref in enumerate(weights_refs):
        low = lax.axis_index("l") ^ step
        spot = (lax.axis_index("h") * LO + low) * Y + lax.axis_index("y")
        begun = starts <= spot
        first = jnp.max(jnp.where(begun, starts, 0))
        count = jnp.min(jnp.where(begun, blocks, starts)) - first
        lhs, rhs = [], []
        for turn in range(turns):
            slot = turn * CLASSES + ((mine - first) & (CLASSES - 1))
            m = jnp.minimum((first + slot) // CLASSES, held - 1)
            rows = jnp.concatenate(
                [blocks_ref[pl.ds(r * held + m, sources, stride=share * held), :] for r in range(share)], axis=0
            )
            lhs.append(jnp.where(slot < count, rows, 0.0))
            rhs.append(jnp.concatenate([weights_ref[mine ^ i, turn] for i in range(CLASSES)], axis=0))
        a_high, a_low = split(jnp.concatenate(lhs, axis=1))
        b_high, b_low = split(jnp.concatenate(rhs, axis=1))
        rows = a_high.shape[0]
        both = dot_nt(jnp.concatenate([a_high, a_low], axis=0), b_high)
        total = both[:rows] + both[rows:] + dot_nt(a_high, b_low)
        for r in range(share):
            out_ref[pl.ds(share * step + r, sources, stride=share * LO), :] = total[r * sources : (r + 1) * sources]


def exchange(pieces, first):
    blocks = pieces.shape[0]
    members = [(first * Y + i) % blocks for i in range(blocks)]
    return lax.all_to_all(
        pieces, VP, split_axis=0, concat_axis=0, tiled=True, axis_index_groups=[members]
    )


def per_device(amplitudes, integrals, rest, occ_energy, vir_energy, block_irrep):
    rows, width = amplitudes.shape
    slots = integrals.shape[1]
    part = integrals.shape[2]
    blocks = block_irrep.shape[0]
    group = blocks // HI
    turns = slots // CLASSES
    held = blocks // CLASSES
    sources = Y * CLASSES
    share = rows // (LO * Y)
    irreps = block_irrep.reshape(1, blocks)

    spread = pl.pallas_call(
        copy_kernel,
        out_shape=jax.ShapeDtypeStruct((HI, rows, width), jnp.float32),
        in_specs=[WHOLE],
        out_specs=WHOLE,
        name="copy_rows",
    )(amplitudes)
    spread = exchange(spread.reshape(blocks, share, width), OUT_FIRST)

    keep, give = pl.pallas_call(
        roll_kernel,
        out_shape=[jax.ShapeDtypeStruct((X, turns, part, width), jnp.float32)] * C,
        in_specs=[WHOLE] * 2,
        out_specs=[WHOLE] * C,
        compiler_params=pltpu.CompilerParams(vmem_limit_bytes=24 * 1024 * 1024),
        name="roll_slots",
    )(irreps, integrals[0])
    cores = jnp.stack([keep, lax.ppermute(give, "c", [(i, i ^ 1) for i in range(C)])], axis=1)
    own = jnp.concatenate(
        [cores[0]] + [lax.ppermute(cores[d], "x", [(i, i ^ d) for i in range(X)]) for d in range(1, X)], axis=0
    )
    far = lax.ppermute(own, "l", [(i, i ^ 2) for i in range(LO)])
    near = lax.ppermute(own, "l", [(i, i ^ 1) for i in range(LO)])
    weights = [own, near, far, lax.ppermute(far, "l", [(i, i ^ 1) for i in range(LO)])]

    by_class = pl.pallas_call(
        functools.partial(spread_kernel, share=share),
        out_shape=jax.ShapeDtypeStruct((Y, CLASSES, share * held, width), jnp.float32),
        in_specs=[WHOLE, WHOLE] + [pl.BlockSpec(memory_space=pl.ANY)] * 2,
        out_specs=WHOLE,
        compiler_params=pltpu.CompilerParams(vmem_limit_bytes=24 * 1024 * 1024),
        name="spread_classes",
    )(irreps, spread.reshape(share * blocks, width), far, near)
    by_class = lax.all_to_all(
        by_class.reshape(sources, share * held, width), PLANE, split_axis=0, concat_axis=0, tiled=True
    )

    partial = pl.pallas_call(
        functools.partial(ladder_kernel, sources=sources, held=held, share=share),
        out_shape=jax.ShapeDtypeStruct((sources * share * LO, width), jnp.float32),
        in_specs=[WHOLE] * (2 + LO),
        out_specs=WHOLE,
        compiler_params=pltpu.CompilerParams(vmem_limit_bytes=24 * 1024 * 1024),
        name="ladder_terms",
    )(irreps, by_class.reshape(sources * share * held, width), *weights)

    partial = lax.all_to_all(
        partial.reshape(sources, share * LO, width), PLANE, split_axis=0, concat_axis=0, tiled=True
    )
    ladder = jnp.sum(partial.reshape(Y, CLASSES, share * LO, width), axis=1).reshape(group, share, width)

    ids = jnp.arange(blocks, dtype=jnp.int32)
    same = block_irrep[:, None] == block_irrep[None, :]
    before = (block_irrep[None, :] < block_irrep[:, None]) | (same & (ids[None, :] < ids[:, None]))
    place = jnp.sum(before.astype(jnp.int32), axis=1)
    local = jnp.clip(place - lax.axis_index("h") * group, 0, group - 1)
    at = (local % Y) * LO + ((local // Y) ^ lax.axis_index("l"))
    at = jnp.roll(at, -HOME_FIRST * Y)
    home = exchange(ladder.at[at].get(mode="promise_in_bounds"), HOME_FIRST)
    place_here = jnp.sum(jnp.where(ids == lax.axis_index(VP), place, 0))
    home = lax.dynamic_index_in_dim(home.reshape(HI, rows, width), (place_here // group - HOME_FIRST // LO) % HI, 0, False)
    return (home + rest) / (vir_energy[None, :] - occ_energy[:, None])


def solution(mesh):
    split_mesh = Mesh(mesh.devices.reshape(HI, LO, Y, X, C), ("h", "l", "y", "x", "c"))
    return jax.shard_map(
        per_device,
        mesh=split_mesh,
        in_specs=(P(OP, VP), P(VP, None, OP, None), P(OP, VP), P(OP), P(VP), P()),
        out_specs=P(OP, VP),
        check_vma=False,
    )
```

```python
import functools

import jax
import jax.numpy as jnp
from jax import lax
from jax.experimental import pallas as pl
from jax.experimental.pallas import tpu as pltpu
from jax.sharding import Mesh, PartitionSpec as P

HI, LO, Y, X, C = 8, 4, 4, 4, 2
IRREPS = 8
CLASSES = X * C
VP = ("h", "l", "y")
OP = ("x", "c")
PLANE = ("y", "x", "c")
OUT_FIRST, HOME_FIRST = 24, 16
WHOLE = pl.BlockSpec(memory_space=pltpu.VMEM)


def starts_of(irreps):
    name = lax.broadcasted_iota(jnp.int32, (IRREPS, irreps.shape[1]), 0)
    return jnp.sum((irreps < name).astype(jnp.int32), axis=1, keepdims=True)


def places_of(irreps):
    blocks = irreps.shape[1]
    own = jnp.broadcast_to(irreps.astype(jnp.float32), (blocks, blocks))
    other = own.T
    own_id = lax.broadcasted_iota(jnp.int32, (blocks, blocks), 1)
    other_id = lax.broadcasted_iota(jnp.int32, (blocks, blocks), 0)
    before = (other < own) | ((other == own) & (other_id < own_id))
    return jnp.sum(before.astype(jnp.float32), axis=0, keepdims=True).astype(jnp.int32)


def pick_rows(chosen, value):
    hot = chosen.astype(jnp.float32).astype(jnp.bfloat16)
    high, rest = split(value)
    low = (value - high.astype(jnp.float32) - rest.astype(jnp.float32)).astype(jnp.bfloat16)
    total = jnp.dot(hot, low, preferred_element_type=jnp.float32)
    total = total + jnp.dot(hot, rest, preferred_element_type=jnp.float32)
    return total + jnp.dot(hot, high, preferred_element_type=jnp.float32)


def copy_kernel(amplitudes_ref, out_ref):
    for hi in range(HI):
        out_ref[hi] = amplitudes_ref[...]


def roll_kernel(irreps_ref, integrals_ref, keep_ref, give_ref):
    starts = starts_of(irreps_ref[...])
    here = lax.axis_index(VP)
    mine = lax.axis_index(OP)
    first = jnp.max(jnp.where(starts <= here, starts, 0))
    for core, out_ref in enumerate((keep_ref, give_ref)):
        for d in range(X):
            slot = ((mine ^ (d * C + core)) - first) & (CLASSES - 1)
            for turn in range(out_ref.shape[1]):
                out_ref[d, turn] = integrals_ref[turn * CLASSES + slot]


def spread_kernel(irreps_ref, blocks_ref, _, __, out_ref, *, share):
    blocks = irreps_ref.shape[1]
    held = blocks // CLASSES
    row = lax.broadcasted_iota(jnp.int32, (blocks, blocks), 0)
    position = (row % held) * CLASSES + row // held
    sources = pltpu.roll(places_of(irreps_ref[...]), blocks - OUT_FIRST * Y, 1)
    chosen = sources == position
    for r in range(share):
        picked = pick_rows(chosen, blocks_ref[pl.ds(r, blocks, stride=share), :]).reshape(CLASSES, held, -1)
        for column in range(Y):
            out_ref[column, :, pl.ds(r * held, held), :] = picked


def split(value):
    high = value.astype(jnp.bfloat16)
    return high, (value - high.astype(jnp.float32)).astype(jnp.bfloat16)


def dot_nt(a, b):
    return lax.dot_general(a, b, (((1,), (1,)), ((), ())), preferred_element_type=jnp.float32)


def ladder_kernel(irreps_ref, blocks_ref, *refs, sources, held, share):
    weights_refs, out_ref = refs[:-1], refs[-1]
    blocks = irreps_ref.shape[1]
    turns, width = weights_refs[0].shape[1], weights_refs[0].shape[3]
    starts = starts_of(irreps_ref[...])
    mine = lax.axis_index(OP)
    for step, weights_ref in enumerate(weights_refs):
        low = lax.axis_index("l") ^ step
        spot = (lax.axis_index("h") * LO + low) * Y + lax.axis_index("y")
        begun = starts <= spot
        first = jnp.max(jnp.where(begun, starts, 0))
        count = jnp.min(jnp.where(begun, blocks, starts)) - first
        lhs, rhs = [], []
        for turn in range(turns):
            slot = turn * CLASSES + ((mine - first) & (CLASSES - 1))
            m = jnp.minimum((first + slot) // CLASSES, held - 1)
            rows = jnp.concatenate(
                [blocks_ref[pl.ds(r * held + m, sources, stride=share * held), :] for r in range(share)], axis=0
            )
            lhs.append(jnp.where(slot < count, rows, 0.0))
            rhs.append(jnp.concatenate([weights_ref[mine ^ i, turn] for i in range(CLASSES)], axis=0))
        a_high, a_low = split(jnp.concatenate(lhs, axis=1))
        b_high, b_low = split(jnp.concatenate(rhs, axis=1))
        rows = a_high.shape[0]
        both = dot_nt(jnp.concatenate([a_high, a_low], axis=0), b_high)
        total = both[:rows] + both[rows:] + dot_nt(a_high, b_low)
        for r in range(share):
            out_ref[pl.ds(share * step + r, sources, stride=share * LO), :] = total[r * sources : (r + 1) * sources]


def exchange(pieces, first):
    blocks = pieces.shape[0]
    members = [(first * Y + i) % blocks for i in range(blocks)]
    return lax.all_to_all(
        pieces, VP, split_axis=0, concat_axis=0, tiled=True, axis_index_groups=[members]
    )


def per_device(amplitudes, integrals, rest, occ_energy, vir_energy, block_irrep):
    rows, width = amplitudes.shape
    slots = integrals.shape[1]
    part = integrals.shape[2]
    blocks = block_irrep.shape[0]
    group = blocks // HI
    turns = slots // CLASSES
    held = blocks // CLASSES
    sources = Y * CLASSES
    share = rows // (LO * Y)
    irreps = block_irrep.reshape(1, blocks)

    spread = pl.pallas_call(
        copy_kernel,
        out_shape=jax.ShapeDtypeStruct((HI, rows, width), jnp.float32),
        in_specs=[WHOLE],
        out_specs=WHOLE,
        name="copy_rows",
    )(amplitudes)
    spread = exchange(spread.reshape(blocks, share, width), OUT_FIRST)

    keep, give = pl.pallas_call(
        roll_kernel,
        out_shape=[jax.ShapeDtypeStruct((X, turns, part, width), jnp.float32)] * C,
        in_specs=[WHOLE] * 2,
        out_specs=[WHOLE] * C,
        compiler_params=pltpu.CompilerParams(vmem_limit_bytes=24 * 1024 * 1024),
        name="roll_slots",
    )(irreps, integrals[0])
    cores = jnp.stack([keep, lax.ppermute(give, "c", [(i, i ^ 1) for i in range(C)])], axis=1)
    own = jnp.concatenate(
        [cores[0]] + [lax.ppermute(cores[d], "x", [(i, i ^ d) for i in range(X)]) for d in range(1, X)], axis=0
    )
    far = lax.ppermute(own, "l", [(i, i ^ 2) for i in range(LO)])
    near = lax.ppermute(own, "l", [(i, i ^ 1) for i in range(LO)])
    weights = [own, near, far, lax.ppermute(far, "l", [(i, i ^ 1) for i in range(LO)])]

    by_class = pl.pallas_call(
        functools.partial(spread_kernel, share=share),
        out_shape=jax.ShapeDtypeStruct((Y, CLASSES, share * held, width), jnp.float32),
        in_specs=[WHOLE, WHOLE] + [pl.BlockSpec(memory_space=pl.ANY)] * 2,
        out_specs=WHOLE,
        compiler_params=pltpu.CompilerParams(vmem_limit_bytes=24 * 1024 * 1024),
        name="spread_classes",
    )(irreps, spread.reshape(share * blocks, width), far, near)
    by_class = lax.all_to_all(
        by_class.reshape(sources, share * held, width), PLANE, split_axis=0, concat_axis=0, tiled=True
    )

    partial = pl.pallas_call(
        functools.partial(ladder_kernel, sources=sources, held=held, share=share),
        out_shape=jax.ShapeDtypeStruct((sources * share * LO, width), jnp.float32),
        in_specs=[WHOLE] * (2 + LO),
        out_specs=WHOLE,
        compiler_params=pltpu.CompilerParams(vmem_limit_bytes=24 * 1024 * 1024),
        name="ladder_terms",
    )(irreps, by_class.reshape(sources * share * held, width), *weights)

    partial = lax.all_to_all(
        partial.reshape(sources, share * LO, width), PLANE, split_axis=0, concat_axis=0, tiled=True
    )
    ladder = jnp.sum(partial.reshape(Y, CLASSES, share * LO, width), axis=1).reshape(group, share, width)

    ids = jnp.arange(blocks, dtype=jnp.int32)
    same = block_irrep[:, None] == block_irrep[None, :]
    before = (block_irrep[None, :] < block_irrep[:, None]) | (same & (ids[None, :] < ids[:, None]))
    place = jnp.sum(before.astype(jnp.int32), axis=1)
    local = jnp.clip(place - lax.axis_index("h") * group, 0, group - 1)
    at = (local % Y) * LO + ((local // Y) ^ lax.axis_index("l"))
    at = jnp.roll(at, -HOME_FIRST * Y)
    home = exchange(ladder.at[at].get(mode="promise_in_bounds"), HOME_FIRST)
    place_here = jnp.sum(jnp.where(ids == lax.axis_index(VP), place, 0))
    home = lax.dynamic_index_in_dim(home.reshape(HI, rows, width), (place_here // group - HOME_FIRST // LO) % HI, 0, False)
    return (home + rest) / (vir_energy[None, :] - occ_energy[:, None])


def solution(mesh):
    split_mesh = Mesh(mesh.devices.reshape(HI, LO, Y, X, C), ("h", "l", "y", "x", "c"))
    return jax.shard_map(
        per_device,
        mesh=split_mesh,
        in_specs=(P(OP, VP), P(VP, None, OP, None), P(OP, VP), P(OP), P(VP), P()),
        out_specs=P(OP, VP),
        check_vma=False,
    )
```

```python
import functools

import jax
import jax.numpy as jnp
from jax import lax
from jax.experimental import pallas as pl
from jax.experimental.pallas import tpu as pltpu
from jax.sharding import Mesh, PartitionSpec as P

HI, LO, Y, X, C = 8, 4, 4, 4, 2
IRREPS = 8
CLASSES = X * C
VP = ("h", "l", "y")
OP = ("x", "c")
PLANE = ("y", "x", "c")
OUT_FIRST, HOME_FIRST = 24, 16
WHOLE = pl.BlockSpec(memory_space=pltpu.VMEM)


def starts_of(irreps):
    name = lax.broadcasted_iota(jnp.int32, (IRREPS, irreps.shape[1]), 0)
    return jnp.sum((irreps < name).astype(jnp.int32), axis=1, keepdims=True)


def places_of(irreps):
    blocks = irreps.shape[1]
    own = jnp.broadcast_to(irreps.astype(jnp.float32), (blocks, blocks))
    other = own.T
    own_id = lax.broadcasted_iota(jnp.int32, (blocks, blocks), 1)
    other_id = lax.broadcasted_iota(jnp.int32, (blocks, blocks), 0)
    before = (other < own) | ((other == own) & (other_id < own_id))
    return jnp.sum(before.astype(jnp.float32), axis=0, keepdims=True).astype(jnp.int32)


def pick_rows(chosen, value):
    hot = chosen.astype(jnp.float32).astype(jnp.bfloat16)
    high, rest = split(value)
    low = (value - high.astype(jnp.float32) - rest.astype(jnp.float32)).astype(jnp.bfloat16)
    total = jnp.dot(hot, low, preferred_element_type=jnp.float32)
    total = total + jnp.dot(hot, rest, preferred_element_type=jnp.float32)
    return total + jnp.dot(hot, high, preferred_element_type=jnp.float32)


def copy_kernel(amplitudes_ref, out_ref):
    for hi in range(HI):
        out_ref[hi] = amplitudes_ref[...]


def roll_kernel(irreps_ref, integrals_ref, keep_ref, give_ref):
    starts = starts_of(irreps_ref[...])
    here = lax.axis_index(VP)
    mine = lax.axis_index(OP)
    first = jnp.max(jnp.where(starts <= here, starts, 0))
    for core, out_ref in enumerate((keep_ref, give_ref)):
        for d in range(X):
            slot = ((mine ^ (d * C + core)) - first) & (CLASSES - 1)
            for turn in range(out_ref.shape[1]):
                out_ref[d, turn] = integrals_ref[turn * CLASSES + slot]


def spread_kernel(irreps_ref, blocks_ref, _, out_ref, *, share):
    blocks = irreps_ref.shape[1]
    held = blocks // CLASSES
    row = lax.broadcasted_iota(jnp.int32, (blocks, blocks), 0)
    position = (row % held) * CLASSES + row // held
    sources = pltpu.roll(places_of(irreps_ref[...]), blocks - OUT_FIRST * Y, 1)
    chosen = sources == position
    for r in range(share):
        picked = pick_rows(chosen, blocks_ref[pl.ds(r, blocks, stride=share), :]).reshape(CLASSES, held, -1)
        for column in range(Y):
            out_ref[column, :, pl.ds(r * held, held), :] = picked


def split(value):
    high = value.astype(jnp.bfloat16)
    return high, (value - high.astype(jnp.float32)).astype(jnp.bfloat16)


def dot_nt(a, b):
    return lax.dot_general(a, b, (((1,), (1,)), ((), ())), preferred_element_type=jnp.float32)


def ladder_kernel(irreps_ref, blocks_ref, *refs, sources, held, share):
    weights_refs, out_ref = refs[:-1], refs[-1]
    blocks = irreps_ref.shape[1]
    turns, width = weights_refs[0].shape[1], weights_refs[0].shape[3]
    starts = starts_of(irreps_ref[...])
    mine = lax.axis_index(OP)
    for step, weights_ref in enumerate(weights_refs):
        low = lax.axis_index("l") ^ step
        spot = (lax.axis_index("h") * LO + low) * Y + lax.axis_index("y")
        begun = starts <= spot
        first = jnp.max(jnp.where(begun, starts, 0))
        count = jnp.min(jnp.where(begun, blocks, starts)) - first
        lhs, rhs = [], []
        for turn in range(turns):
            slot = turn * CLASSES + ((mine - first) & (CLASSES - 1))
            m = jnp.minimum((first + slot) // CLASSES, held - 1)
            rows = jnp.concatenate(
                [blocks_ref[pl.ds(r * held + m, sources, stride=share * held), :] for r in range(share)], axis=0
            )
            lhs.append(jnp.where(slot < count, rows, 0.0))
            rhs.append(jnp.concatenate([weights_ref[mine ^ i, turn] for i in range(CLASSES)], axis=0))
        a_high, a_low = split(jnp.concatenate(lhs, axis=1))
        b_high, b_low = split(jnp.concatenate(rhs, axis=1))
        rows = a_high.shape[0]
        both = dot_nt(jnp.concatenate([a_high, a_low], axis=0), b_high)
        total = both[:rows] + both[rows:] + dot_nt(a_high, b_low)
        for r in range(share):
            out_ref[pl.ds(share * step + r, sources, stride=share * LO), :] = total[r * sources : (r + 1) * sources]


def exchange(pieces, first):
    blocks = pieces.shape[0]
    members = [(first * Y + i) % blocks for i in range(blocks)]
    return lax.all_to_all(
        pieces, VP, split_axis=0, concat_axis=0, tiled=True, axis_index_groups=[members]
    )


def per_device(amplitudes, integrals, rest, occ_energy, vir_energy, block_irrep):
    rows, width = amplitudes.shape
    slots = integrals.shape[1]
    part = integrals.shape[2]
    blocks = block_irrep.shape[0]
    group = blocks // HI
    turns = slots // CLASSES
    held = blocks // CLASSES
    sources = Y * CLASSES
    share = rows // (LO * Y)
    irreps = block_irrep.reshape(1, blocks)

    spread = pl.pallas_call(
        copy_kernel,
        out_shape=jax.ShapeDtypeStruct((HI, rows, width), jnp.float32),
        in_specs=[WHOLE],
        out_specs=WHOLE,
        name="copy_rows",
    )(amplitudes)
    spread = exchange(spread.reshape(blocks, share, width), OUT_FIRST)

    keep, give = pl.pallas_call(
        roll_kernel,
        out_shape=[jax.ShapeDtypeStruct((X, turns, part, width), jnp.float32)] * C,
        in_specs=[WHOLE] * 2,
        out_specs=[WHOLE] * C,
        compiler_params=pltpu.CompilerParams(vmem_limit_bytes=24 * 1024 * 1024),
        name="roll_slots",
    )(irreps, integrals[0])
    cores = jnp.stack([keep, lax.ppermute(give, "c", [(i, i ^ 1) for i in range(C)])], axis=1)
    own = jnp.concatenate(
        [cores[0]] + [lax.ppermute(cores[d], "x", [(i, i ^ d) for i in range(X)]) for d in range(1, X)], axis=0
    )
    far = lax.ppermute(own, "l", [(i, i ^ 2) for i in range(LO)])
    near = lax.ppermute(own, "l", [(i, i ^ 1) for i in range(LO)])
    weights = [own, near, far, lax.ppermute(far, "l", [(i, i ^ 1) for i in range(LO)])]

    by_class = pl.pallas_call(
        functools.partial(spread_kernel, share=share),
        out_shape=jax.ShapeDtypeStruct((Y, CLASSES, share * held, width), jnp.float32),
        in_specs=[WHOLE, WHOLE, pl.BlockSpec(memory_space=pl.ANY)],
        out_specs=WHOLE,
        compiler_params=pltpu.CompilerParams(vmem_limit_bytes=24 * 1024 * 1024),
        name="spread_classes",
    )(irreps, spread.reshape(share * blocks, width), far)
    by_class = lax.all_to_all(
        by_class.reshape(sources, share * held, width), PLANE, split_axis=0, concat_axis=0, tiled=True
    )

    partial = pl.pallas_call(
        functools.partial(ladder_kernel, sources=sources, held=held, share=share),
        out_shape=jax.ShapeDtypeStruct((sources * share * LO, width), jnp.float32),
        in_specs=[WHOLE] * (2 + LO),
        out_specs=WHOLE,
        compiler_params=pltpu.CompilerParams(vmem_limit_bytes=24 * 1024 * 1024),
        name="ladder_terms",
    )(irreps, by_class.reshape(sources * share * held, width), *weights)

    partial = lax.all_to_all(
        partial.reshape(sources, share * LO, width), PLANE, split_axis=0, concat_axis=0, tiled=True
    )
    ladder = jnp.sum(partial.reshape(Y, CLASSES, share * LO, width), axis=1).reshape(group, share, width)

    ids = jnp.arange(blocks, dtype=jnp.int32)
    same = block_irrep[:, None] == block_irrep[None, :]
    before = (block_irrep[None, :] < block_irrep[:, None]) | (same & (ids[None, :] < ids[:, None]))
    place = jnp.sum(before.astype(jnp.int32), axis=1)
    local = jnp.clip(place - lax.axis_index("h") * group, 0, group - 1)
    at = (local % Y) * LO + ((local // Y) ^ lax.axis_index("l"))
    at = jnp.roll(at, -HOME_FIRST * Y)
    home = exchange(ladder.at[at].get(mode="promise_in_bounds"), HOME_FIRST)
    place_here = jnp.sum(jnp.where(ids == lax.axis_index(VP), place, 0))
    home = lax.dynamic_index_in_dim(home.reshape(HI, rows, width), (place_here // group - HOME_FIRST // LO) % HI, 0, False)
    return (home + rest) / (vir_energy[None, :] - occ_energy[:, None])


def solution(mesh):
    split_mesh = Mesh(mesh.devices.reshape(HI, LO, Y, X, C), ("h", "l", "y", "x", "c"))
    return jax.shard_map(
        per_device,
        mesh=split_mesh,
        in_specs=(P(OP, VP), P(VP, None, OP, None), P(OP, VP), P(OP), P(VP), P()),
        out_specs=P(OP, VP),
        check_vma=False,
    )
```

```python
import functools

import jax
import jax.numpy as jnp
from jax import lax
from jax.experimental import pallas as pl
from jax.experimental.pallas import tpu as pltpu
from jax.sharding import Mesh, PartitionSpec as P

HI, LO, Y, X, C = 8, 4, 4, 4, 2
IRREPS = 8
CLASSES = X * C
VP = ("h", "l", "y")
OP = ("x", "c")
PLANE = ("y", "x", "c")
OUT_FIRST, HOME_FIRST = 24, 20
WHOLE = pl.BlockSpec(memory_space=pltpu.VMEM)


def starts_of(irreps):
    name = lax.broadcasted_iota(jnp.int32, (IRREPS, irreps.shape[1]), 0)
    return jnp.sum((irreps < name).astype(jnp.int32), axis=1, keepdims=True)


def places_of(irreps):
    blocks = irreps.shape[1]
    own = jnp.broadcast_to(irreps.astype(jnp.float32), (blocks, blocks))
    other = own.T
    own_id = lax.broadcasted_iota(jnp.int32, (blocks, blocks), 1)
    other_id = lax.broadcasted_iota(jnp.int32, (blocks, blocks), 0)
    before = (other < own) | ((other == own) & (other_id < own_id))
    return jnp.sum(before.astype(jnp.float32), axis=0, keepdims=True).astype(jnp.int32)


def pick_rows(chosen, value):
    hot = chosen.astype(jnp.float32).astype(jnp.bfloat16)
    high, rest = split(value)
    low = (value - high.astype(jnp.float32) - rest.astype(jnp.float32)).astype(jnp.bfloat16)
    total = jnp.dot(hot, low, preferred_element_type=jnp.float32)
    total = total + jnp.dot(hot, rest, preferred_element_type=jnp.float32)
    return total + jnp.dot(hot, high, preferred_element_type=jnp.float32)


def copy_kernel(amplitudes_ref, out_ref):
    for hi in range(HI):
        out_ref[hi] = amplitudes_ref[...]


def roll_kernel(irreps_ref, integrals_ref, keep_ref, give_ref):
    starts = starts_of(irreps_ref[...])
    here = lax.axis_index(VP)
    mine = lax.axis_index(OP)
    first = jnp.max(jnp.where(starts <= here, starts, 0))
    for core, out_ref in enumerate((keep_ref, give_ref)):
        for d in range(X):
            slot = ((mine ^ (d * C + core)) - first) & (CLASSES - 1)
            for turn in range(out_ref.shape[1]):
                out_ref[d, turn] = integrals_ref[turn * CLASSES + slot]


def spread_kernel(irreps_ref, blocks_ref, _, __, out_ref, *, share):
    blocks = irreps_ref.shape[1]
    held = blocks // CLASSES
    row = lax.broadcasted_iota(jnp.int32, (blocks, blocks), 0)
    position = (row % held) * CLASSES + row // held
    sources = pltpu.roll(places_of(irreps_ref[...]), blocks - OUT_FIRST * Y, 1)
    chosen = sources == position
    for r in range(share):
        picked = pick_rows(chosen, blocks_ref[pl.ds(r, blocks, stride=share), :]).reshape(CLASSES, held, -1)
        for column in range(Y):
            out_ref[column, :, pl.ds(r * held, held), :] = picked


def split(value):
    high = value.astype(jnp.bfloat16)
    return high, (value - high.astype(jnp.float32)).astype(jnp.bfloat16)


def dot_nt(a, b):
    return lax.dot_general(a, b, (((1,), (1,)), ((), ())), preferred_element_type=jnp.float32)


def ladder_kernel(irreps_ref, blocks_ref, *refs, sources, held, share):
    weights_refs, out_ref = refs[:-1], refs[-1]
    blocks = irreps_ref.shape[1]
    turns, width = weights_refs[0].shape[1], weights_refs[0].shape[3]
    starts = starts_of(irreps_ref[...])
    mine = lax.axis_index(OP)
    for step, weights_ref in enumerate(weights_refs):
        low = lax.axis_index("l") ^ step
        spot = (lax.axis_index("h") * LO + low) * Y + lax.axis_index("y")
        begun = starts <= spot
        first = jnp.max(jnp.where(begun, starts, 0))
        count = jnp.min(jnp.where(begun, blocks, starts)) - first
        lhs, rhs = [], []
        for turn in range(turns):
            slot = turn * CLASSES + ((mine - first) & (CLASSES - 1))
            m = jnp.minimum((first + slot) // CLASSES, held - 1)
            rows = jnp.concatenate(
                [blocks_ref[pl.ds(r * held + m, sources, stride=share * held), :] for r in range(share)], axis=0
            )
            lhs.append(jnp.where(slot < count, rows, 0.0))
            rhs.append(jnp.concatenate([weights_ref[mine ^ i, turn] for i in range(CLASSES)], axis=0))
        a_high, a_low = split(jnp.concatenate(lhs, axis=1))
        b_high, b_low = split(jnp.concatenate(rhs, axis=1))
        rows = a_high.shape[0]
        both = dot_nt(jnp.concatenate([a_high, a_low], axis=0), b_high)
        total = both[:rows] + both[rows:] + dot_nt(a_high, b_low)
        for r in range(share):
            out_ref[pl.ds(share * step + r, sources, stride=share * LO), :] = total[r * sources : (r + 1) * sources]


def exchange(pieces, first):
    blocks = pieces.shape[0]
    members = [(first * Y + i) % blocks for i in range(blocks)]
    return lax.all_to_all(
        pieces, VP, split_axis=0, concat_axis=0, tiled=True, axis_index_groups=[members]
    )


def per_device(amplitudes, integrals, rest, occ_energy, vir_energy, block_irrep):
    rows, width = amplitudes.shape
    slots = integrals.shape[1]
    part = integrals.shape[2]
    blocks = block_irrep.shape[0]
    group = blocks // HI
    turns = slots // CLASSES
    held = blocks // CLASSES
    sources = Y * CLASSES
    share = rows // (LO * Y)
    irreps = block_irrep.reshape(1, blocks)

    spread = pl.pallas_call(
        copy_kernel,
        out_shape=jax.ShapeDtypeStruct((HI, rows, width), jnp.float32),
        in_specs=[WHOLE],
        out_specs=WHOLE,
        name="copy_rows",
    )(amplitudes)
    spread = exchange(spread.reshape(blocks, share, width), OUT_FIRST)

    keep, give = pl.pallas_call(
        roll_kernel,
        out_shape=[jax.ShapeDtypeStruct((X, turns, part, width), jnp.float32)] * C,
        in_specs=[WHOLE] * 2,
        out_specs=[WHOLE] * C,
        compiler_params=pltpu.CompilerParams(vmem_limit_bytes=24 * 1024 * 1024),
        name="roll_slots",
    )(irreps, integrals[0])
    cores = jnp.stack([keep, lax.ppermute(give, "c", [(i, i ^ 1) for i in range(C)])], axis=1)
    own = jnp.concatenate(
        [cores[0]] + [lax.ppermute(cores[d], "x", [(i, i ^ d) for i in range(X)]) for d in range(1, X)], axis=0
    )
    far = lax.ppermute(own, "l", [(i, i ^ 2) for i in range(LO)])
    near = lax.ppermute(own, "l", [(i, i ^ 1) for i in range(LO)])
    weights = [own, near, far, lax.ppermute(far, "l", [(i, i ^ 1) for i in range(LO)])]

    by_class = pl.pallas_call(
        functools.partial(spread_kernel, share=share),
        out_shape=jax.ShapeDtypeStruct((Y, CLASSES, share * held, width), jnp.float32),
        in_specs=[WHOLE, WHOLE] + [pl.BlockSpec(memory_space=pl.ANY)] * 2,
        out_specs=WHOLE,
        compiler_params=pltpu.CompilerParams(vmem_limit_bytes=24 * 1024 * 1024),
        name="spread_classes",
    )(irreps, spread.reshape(share * blocks, width), far, near)
    by_class = lax.all_to_all(
        by_class.reshape(sources, share * held, width), PLANE, split_axis=0, concat_axis=0, tiled=True
    )

    partial = pl.pallas_call(
        functools.partial(ladder_kernel, sources=sources, held=held, share=share),
        out_shape=jax.ShapeDtypeStruct((sources * share * LO, width), jnp.float32),
        in_specs=[WHOLE] * (2 + LO),
        out_specs=WHOLE,
        compiler_params=pltpu.CompilerParams(vmem_limit_bytes=24 * 1024 * 1024),
        name="ladder_terms",
    )(irreps, by_class.reshape(sources * share * held, width), *weights)

    partial = lax.all_to_all(
        partial.reshape(sources, share * LO, width), PLANE, split_axis=0, concat_axis=0, tiled=True
    )
    ladder = jnp.sum(partial.reshape(Y, CLASSES, share * LO, width), axis=1).reshape(group, share, width)

    ids = jnp.arange(blocks, dtype=jnp.int32)
    same = block_irrep[:, None] == block_irrep[None, :]
    before = (block_irrep[None, :] < block_irrep[:, None]) | (same & (ids[None, :] < ids[:, None]))
    place = jnp.sum(before.astype(jnp.int32), axis=1)
    local = jnp.clip(place - lax.axis_index("h") * group, 0, group - 1)
    at = (local % Y) * LO + ((local // Y) ^ lax.axis_index("l"))
    at = jnp.roll(at, -HOME_FIRST * Y)
    home = exchange(ladder.at[at].get(mode="promise_in_bounds"), HOME_FIRST)
    place_here = jnp.sum(jnp.where(ids == lax.axis_index(VP), place, 0))
    home = lax.dynamic_index_in_dim(home.reshape(HI, rows, width), (place_here // group - HOME_FIRST // LO) % HI, 0, False)
    return (home + rest) / (vir_energy[None, :] - occ_energy[:, None])


def solution(mesh):
    split_mesh = Mesh(mesh.devices.reshape(HI, LO, Y, X, C), ("h", "l", "y", "x", "c"))
    return jax.shard_map(
        per_device,
        mesh=split_mesh,
        in_specs=(P(OP, VP), P(VP, None, OP, None), P(OP, VP), P(OP), P(VP), P()),
        out_specs=P(OP, VP),
        check_vma=False,
    )
```
